512 devices in a mesh: rows: 256 (over x, z, y), cols: 2 (over core).
Axes of the slice: x: 4, y: 8, z: 8, core: 2. Of those that a mesh axis runs over, the one named last changes fastest.
Arguments:
- row_points: float32 [3, 131072], P(None, 'rows')
- panel_points: bfloat16 [3, 8192], P(None, ('rows', 'cols')), may hold values from 0 to 1
- test_vectors: bfloat16 [128, 8192], P(None, ('rows', 'cols')), may hold values from -0.0625 to 0.0625
- leaf_skeleton: int32 [256, 64], P('rows'), may hold values from 0 to 511, as said below
- node_skeleton: int32 [256, 4, 64], P('rows'), may hold values from 0 to 127, as said below
Outputs:
- leaf_interp: float32 [64, 131072], P(None, ('rows', 'cols'))
- transfers: float32 [256, 4, 64, 128], P('rows')
- top_skeleton: float32 [256, 64, 256], P('rows')
The draws below stay inside these ranges and needn't reach their ends.
Inputs may be any that keep to these rules, and one draw needn't show every extreme that they name: `leaf_skeleton`: each leaf's 64 entries are distinct. `node_skeleton`: each entry list holds 64 distinct positions among the 128 stacked rows (the lower child's first); all leaves under the same node have the same list at that level.
All inputs are finite; a program needn't handle non-finite values.
Results may differ from the reference program's by a relative error of at most 0.0049.
Values may be sent and summed in bfloat16 or wider, within the bound.
A program may use at most 64 MiB of HBM per device.

```python
import jax
import jax.numpy as jnp
from jax import lax

ROWS_DEV = 512
R = 128
K = 64
LEVELS = 4
LEAVES = 256
N = 131072
PANEL = 8192


def draw_row_points(key, part):
    leaf_ids = (jnp.arange(N) // ROWS_DEV).astype(jnp.float32)
    jitter = jax.random.uniform(jax.random.fold_in(key, 3), (3, N), jnp.float32)
    along_x = (leaf_ids + jitter[0]) / LEAVES
    return jnp.stack([along_x, jitter[1], jitter[2]])


def leaf_pick(one_key):
    return jax.random.permutation(one_key, ROWS_DEV)[:K]


def node_pick(one_key):
    return jax.random.permutation(one_key, 2 * K)[:K]


def draw_leaf_skeleton(key, part):
    key_list = jax.random.split(jax.random.fold_in(key, 5), LEAVES)
    return jax.vmap(leaf_pick)(key_list).astype(jnp.int32)


def draw_node_skeleton(key, part):
    key_list = jax.random.split(jax.random.fold_in(key, 7), LEVELS * LEAVES)
    node_table = jax.vmap(node_pick)(key_list).reshape(LEVELS, LEAVES, K)
    leaf_ids = jnp.arange(LEAVES)
    row_sets = [node_table[tree_level][jnp.right_shift(leaf_ids, tree_level + 1)] for tree_level in range(LEVELS)]
    return jnp.stack(row_sets, axis=1).astype(jnp.int32)


def shard_levels(rng, extent, cuts, low, high):
    def one(axis_at, blocks):
        draws = jax.random.uniform(jax.random.fold_in(jax.random.fold_in(rng, 6), axis_at), (blocks,), jnp.float32, low / len(cuts), high / len(cuts))
        return jnp.repeat(jnp.exp(draws), extent[axis_at] // blocks).reshape((-1,) + (1,) * (len(extent) - axis_at - 1))

    factor_of = one(*cuts[0])
    for cut in cuts[1:]:
        factor_of = factor_of * one(*cut)
    return factor_of


def bell_draw(rng, dims, width, bound, pieces=(), kind=jnp.bfloat16):
    drawn = width * jax.random.normal(rng, dims, jnp.float32)
    if pieces:
        drawn = drawn * shard_levels(rng, dims, pieces, -0.22, 0.18)
    return jnp.clip(drawn, -bound, bound).astype(kind)


def setup_inputs(seed: int = 0) -> dict:
    streams_of = jax.random.split(jax.random.key(seed), 6)
    return {
        "row_points": draw_row_points(jax.random.fold_in(streams_of[5], 71), 0),
        "panel_points": jnp.clip(1.0 * jax.random.uniform(streams_of[1], (3, PANEL), jnp.float32) ** shard_levels(streams_of[1], (3, PANEL), ((1, 512),), -0.2, 0.2), 0.0, 1.0).astype(jnp.bfloat16),
        "test_vectors": bell_draw(streams_of[2], (R, PANEL), PANEL ** -0.5, 0.0625, ((1, 512),)),
        "leaf_skeleton": draw_leaf_skeleton(jax.random.fold_in(streams_of[5], 71), 0),
        "node_skeleton": draw_node_skeleton(jax.random.fold_in(streams_of[5], 71), 0),
    }


KAPPA = 40.0
SMOOTH = 0.05
RIDGE = 0.1
EPSILON = 1e-05

def kernel_block(targets, sources):
    source_f = sources.astype(jnp.float32)
    dist_sq = jnp.zeros((targets.shape[1], source_f.shape[1]), jnp.float32)
    for component in range(3):
        offset = targets[component][:, None] - source_f[component][None, :]
        dist_sq = dist_sq + offset * offset
    radius = jnp.sqrt(dist_sq + SMOOTH * SMOOTH)
    real_part = (jnp.cos(KAPPA * radius) / radius).astype(jnp.bfloat16)
    imag_part = (jnp.sin(KAPPA * radius) / radius).astype(jnp.bfloat16)
    return (real_part, imag_part)

def sample_block(real_part, imag_part, vectors):
    first_half = jnp.dot(real_part.astype(jnp.float32), vectors.T.astype(jnp.float32), preferred_element_type=jnp.float32)
    second_half = jnp.dot(imag_part.astype(jnp.float32), vectors.T.astype(jnp.float32), preferred_element_type=jnp.float32)
    return jnp.concatenate([first_half, second_half], axis=1)

def interpolate(block, skeleton):
    gram_matrix = jnp.dot(skeleton, skeleton.T, precision=lax.Precision.HIGHEST)
    ridge = RIDGE * skeleton.shape[1] * (jnp.mean(skeleton * skeleton) + EPSILON)
    gram_matrix = gram_matrix + ridge * jnp.eye(skeleton.shape[0], dtype=skeleton.dtype)
    factor = jnp.linalg.cholesky(gram_matrix)
    right_side = jnp.dot(skeleton, block.T, precision=lax.Precision.HIGHEST)
    middle = lax.linalg.triangular_solve(factor, right_side, left_side=True, lower=True)
    return lax.linalg.triangular_solve(factor, middle, left_side=True, lower=True, transpose_a=True)

def reference(row_points, panel_points, test_vectors, leaf_skeleton, node_skeleton):

    def leaf_samples(targets):
        real_part, imag_part = kernel_block(targets, panel_points)
        return sample_block(real_part, imag_part, test_vectors)
    blocks = row_points.reshape(3, LEAVES, ROWS_DEV).transpose(1, 0, 2)
    samples = lax.map(leaf_samples, blocks)
    current = jnp.take_along_axis(samples, leaf_skeleton[:, :, None], axis=1)
    leaf_maps = jax.vmap(interpolate)(samples, current)
    leaf_interp = leaf_maps.transpose(1, 0, 2).reshape(K, N)
    level_maps = []
    for tree_level in range(LEVELS):
        nodes = current.shape[0] // 2
        stacked = current.reshape(nodes, 2 * K, current.shape[2])
        chosen = node_skeleton[::2 ** (tree_level + 1), tree_level, :]
        current = jnp.take_along_axis(stacked, chosen[:, :, None], axis=1)
        transfer_maps = jax.vmap(interpolate)(stacked, current)
        level_maps.append(jnp.repeat(transfer_maps, 2 ** (tree_level + 1), axis=0))
    transfers = jnp.stack(level_maps, axis=1)
    top_skeleton = jnp.repeat(current, 2 ** LEVELS, axis=0)
    return (leaf_interp, transfers, top_skeleton)
```

```python
import functools
import math

import jax
import jax.numpy as jnp
from jax import lax
from jax.experimental import pallas as pl
from jax.experimental.pallas import tpu as pltpu
from jax.sharding import PartitionSpec as P

KAPPA = 40.0
SMOOTH = 0.05
RIDGE = 0.1
EPSILON = 1e-05

MESH = pl.DeviceIdType.MESH
HI = lax.Precision.HIGHEST
NT = (((1,), (1,)), ((), ()))
F32 = jnp.float32
BF16 = jnp.bfloat16

NX, NZ, NY = 4, 8, 8
LEAF = 512
VEC = 128
SK = 64
LEVELS = 4
TREE = LEVELS * SK
ROWS = LEAF + TREE
HALF = LEAF // 2
POOL = HALF + SK + TREE
UNIT = 256
GROUPS = ((0, 8),)

TURNS = KAPPA / (2.0 * math.pi)
SIN_C = (4.442867902958649, -7.307443418384947, 3.5947880506885697, -0.7843739567847821)
COS_C = (1.41421349656788, -6.97885098835421, 5.739461171797141, -1.8835629903414894, 0.3106981920345144)


def horner(q, coefs):
    out = q * coefs[-1] + coefs[-2]
    for c in coefs[-3::-1]:
        out = out * q + c
    return out


def kernel_values(dist_sq):
    inv = lax.rsqrt(dist_sq)
    turns = (dist_sq * inv) * TURNS
    frac = turns - jnp.round(turns)
    q = frac * frac
    sin_half = horner(q, SIN_C) * frac
    cos_half = horner(q, COS_C)
    scaled = inv * sin_half
    return (inv - scaled * sin_half).astype(BF16), (scaled * cos_half).astype(BF16)


def split3(v):
    hi = v.astype(BF16).astype(F32)
    mid = (v - hi).astype(BF16).astype(F32)
    lo = (v - hi - mid).astype(BF16).astype(F32)
    return hi, mid, lo


def stack_rows(rows, width):
    idx = lax.broadcasted_iota(jnp.int32, (16, width), 0)
    out = jnp.zeros((16, width), F32)
    for i, r in enumerate(rows):
        out = jnp.where(idx == i, jnp.broadcast_to(r, (16, width)), out)
    return out


def source_features(points):
    y = [points[i : i + 1, :] for i in range(3)]
    norm = split3(y[0] * y[0] + y[1] * y[1] + y[2] * y[2])
    one = jnp.ones_like(y[0])
    return stack_rows(y * 3 + list(norm) + [one] * 3, points.shape[1])


def target_features(points):
    x = [points[i : i + 1, :] for i in range(3)]
    parts = [split3(-2.0 * v) for v in x]
    norm = split3(x[0] * x[0] + x[1] * x[1] + x[2] * x[2] + SMOOTH * SMOOTH)
    one = jnp.ones_like(x[0])
    rows = [parts[k][s] for s in range(3) for k in range(3)]
    return stack_rows(rows + [one] * 3 + list(norm), points.shape[1])


def target_rows(points):
    feats = target_features(points)
    return jnp.concatenate([feats] * 8, axis=0).T.astype(BF16)


def pick_points(points, picks):
    n = points.shape[1]
    hot = lax.broadcasted_iota(jnp.int32, (n, SK), 0) == picks
    return jnp.dot(points, hot.astype(F32), precision=HI, preferred_element_type=F32)


def group_rows(g):
    return (GROUPS[g][1] + 1) * 16


def group_base(g):
    return sum(32 * group_rows(i) for i in range(g))


def ring_dist(t, n):
    return min(t % n, -t % n)


LINE = (4, 3, 5, 2, 6, 1, 7)
PLANE = sorted(
    [(i, k) for i in range(NX) for k in range(NZ) if (i, k) != (0, 0)],
    key=lambda t: ring_dist(t[0], NX) + ring_dist(t[1], NZ),
)


def sample_kernel(
    pts_ref, panel_ref, vec_ref, lskel_ref, nskel_ref, lskel_s, out_ref,
    raw, gath, tgt, u_s, k_re, k_im, acc, own_s, swap_tx, swap_rx, rx,
    raw_send, raw_recv, g_send, g_recv, t_send, t_recv, x_send, x_recv,
):
    row = lax.axis_index("rows")
    col = lax.axis_index("cols")
    x, z, y = row // 64, (row // 8) % 8, row % 8
    first = col == 0
    a = jnp.where(first, y, z)
    b = jnp.where(first, z, y)
    step_a = jnp.where(first, 1, 8)
    step_b = jnp.where(first, 8, 1)

    def on_line(j):
        return {"rows": row + ((a + j) % 8 - a) * step_a}

    def on_plane(i, k):
        return {"rows": row + ((x + i) % 4 - x) * 64 + ((b + k) % 8 - b) * step_b}

    barrier = pltpu.get_barrier_semaphore()
    peers = [on_line(j) for j in LINE] + [on_plane(*t) for t in PLANE] + [{"cols": 1 - col}]
    for peer in peers:
        pl.semaphore_signal(barrier, inc=1, device_id=peer, device_id_type=MESH)

    eye = (
        lax.broadcasted_iota(jnp.int32, (16, 16), 0) == lax.broadcasted_iota(jnp.int32, (16, 16), 1)
    ).astype(BF16)
    mine = pl.ds(pl.multiple_of(a * 32, 32), 16)
    mine_f = pl.ds(pl.multiple_of(a * 32 + 16, 16), 16)
    mine_both = pl.ds(pl.multiple_of(a * 32, 32), 32)
    raw[mine] = lax.dot_general(eye, vec_ref[...], NT, preferred_element_type=F32).astype(BF16)
    feats = jnp.concatenate([source_features(panel_ref[...].astype(F32))] * 8, axis=0)
    slot = lax.broadcasted_iota(jnp.int32, (128, 16), 0) // 16
    feats = jnp.where(slot == a, feats, 0.0).astype(BF16)
    raw[mine_f] = lax.dot_general(eye, feats, NT, preferred_element_type=F32).astype(BF16)

    pl.semaphore_wait(barrier, len(peers))

    for j in LINE:
        pltpu.make_async_remote_copy(
            raw.at[mine_both], raw.at[mine_both], raw_send, raw_recv.at[j], device_id=on_line(j), device_id_type=MESH
        ).start()

    zero_row = jnp.zeros((5, LEAF), F32)
    points = jnp.concatenate([pts_ref[...], zero_row], axis=0)
    current = pick_points(points, lskel_ref[...])

    def swap_copy(lev):
        bit = (row // (1 << lev)) % 2
        return pltpu.make_async_remote_copy(
            swap_tx.at[lev], swap_rx.at[lev], t_send.at[lev], t_recv.at[lev],
            device_id={"rows": row + (1 - 2 * bit) * (1 << lev)}, device_id_type=MESH,
        )

    def swap_start(lev, cur):
        bit = (row // (1 << lev)) % 2
        wide = jnp.concatenate([cur, cur], axis=1)
        upper = lax.broadcasted_iota(jnp.int32, (8, 2 * SK), 1) // SK
        swap_tx[lev] = jnp.where(upper == bit, wide, 0.0)
        swap_copy(lev).start()

    def swap_finish(lev):
        swap_copy(lev).wait_recv()
        bit = (row // (1 << lev)) % 2
        got = swap_rx[lev]
        other = jnp.where(bit == 1, got[:, :SK], got[:, SK:])
        tgt[LEAF + lev * SK : LEAF + (lev + 1) * SK] = target_rows(other)
        both = swap_tx[lev] + got
        return pick_points(both, nskel_ref[lev : lev + 1, :])

    swap_start(0, current)
    tgt[0:LEAF] = target_rows(pts_ref[...])
    acc[...] = jnp.zeros_like(acc)

    def block_copy(g, n, i, k):
        rows = group_rows(g)
        base = group_base(g)
        return pltpu.make_async_remote_copy(
            gath.at[pl.ds(base, rows)], gath.at[pl.ds(base + n * rows, rows)], g_send.at[g], g_recv.at[g, n],
            device_id=on_plane(i, k), device_id_type=MESH,
        )

    def send_group(g):
        start, count = GROUPS[g]
        base = group_base(g)
        for j in range(1, 8):
            src = (a + 8 - j) % 8
            needed = jnp.logical_and(src >= start, src < start + count)

            @pl.when(needed)
            def _():
                pltpu.make_async_remote_copy(
                    raw.at[mine_both], raw.at[mine_both], raw_send, raw_recv.at[j], device_id=on_line(j), device_id_type=MESH
                ).wait_recv()

        feat = jnp.zeros((16, 128), BF16)
        for i in range(count):
            at = (start + i) * 32
            gath[base + 16 * i : base + 16 * i + 16] = raw[at : at + 16]
            feat = feat + raw[at + 16 : at + 32]
        gath[base + 16 * count : base + 16 * count + 16] = feat
        for n, (i, k) in enumerate(PLANE):
            block_copy(g, n + 1, i, k).start()

    lane = lax.broadcasted_iota(jnp.int32, (16, 128), 1) // 16

    def compute_unit(g, unit):
        start, count = GROUPS[g]
        rows = group_rows(g)
        srcs = UNIT // (16 * count)
        vecs, feats = [], []
        for s in range(srcs):
            n = unit * srcs + s

            @pl.when(n > 0)
            def _():
                block_copy(g, n, 0, 1).wait_recv()

            at = group_base(g) + n * rows
            vecs.append(gath[pl.ds(pl.multiple_of(at, 16), 16 * count)])
            tile = gath[pl.ds(pl.multiple_of(at + 16 * count, 16), 16)]
            for j in range(start, start + count):
                feats.append(jnp.where(lane == j, tile, jnp.zeros_like(tile)))
        feat = jnp.concatenate(feats, axis=0)
        vec = jnp.concatenate(vecs, axis=0)
        u_s[...] = lax.dot_general(tgt[...], feat, NT, preferred_element_type=F32)
        for r in range(0, ROWS, 32):
            re, im = kernel_values(u_s[r : r + 32])
            k_re[r : r + 32] = re
            k_im[r : r + 32] = im
        acc[:, :VEC] += jnp.dot(k_re[...], vec, preferred_element_type=F32)
        acc[:, VEC:] += jnp.dot(k_im[...], vec, preferred_element_type=F32)

    for g in range(len(GROUPS)):
        send_group(g)
    for lev in range(LEVELS):
        current = swap_finish(lev)
        if lev + 1 < LEVELS:
            swap_start(lev + 1, current)
    for g in range(len(GROUPS)):
        units = 32 * 16 * GROUPS[g][1] // UNIT

        def step(u, carry, g=g):
            compute_unit(g, u)
            return carry

        lax.fori_loop(0, units, step, 0)

    for k in range(SK):
        own_s[k : k + 1] = acc[pl.ds(lskel_s[0, k], 1)]
    theirs = pl.ds(pl.multiple_of((1 - col) * HALF, HALF), HALF)
    ours = pl.ds(pl.multiple_of(col * HALF, HALF), HALF)
    spans = (
        (acc.at[theirs], rx.at[pl.ds(0, HALF)]),
        (own_s, rx.at[pl.ds(HALF, SK)]),
        (acc.at[pl.ds(LEAF, TREE)], rx.at[pl.ds(HALF + SK, TREE)]),
    )
    copies = [
        pltpu.make_async_remote_copy(
            src, dst, x_send.at[i], x_recv.at[i], device_id={"cols": 1 - col}, device_id_type=MESH
        )
        for i, (src, dst) in enumerate(spans)
    ]
    for c in copies:
        c.start()
    for c in copies:
        c.wait_recv()
    out_ref[0:HALF] = acc[ours] + rx[0:HALF]
    out_ref[HALF : HALF + SK] = own_s[...] + rx[HALF : HALF + SK]
    out_ref[HALF + SK : POOL] = acc[LEAF:ROWS] + rx[HALF + SK : POOL]

    for c in copies:
        c.wait_send()
    for lev in range(LEVELS):
        swap_copy(lev).wait_send()
    for j in LINE:
        pltpu.make_async_remote_copy(
            raw.at[mine_both], raw.at[mine_both], raw_send, raw_recv.at[j], device_id=on_line(j), device_id_type=MESH
        ).wait_send()
    for g in range(len(GROUPS)):
        for n, (i, k) in enumerate(PLANE):
            block_copy(g, n + 1, i, k).wait_send()


def sample_rows(row_points, panel_points, test_vectors, leaf_skeleton, node_skeleton):
    vmem = pl.BlockSpec(memory_space=pltpu.VMEM)
    n_groups = len(GROUPS)
    gath_rows = group_base(n_groups)
    dma = pltpu.SemaphoreType.DMA
    return pl.pallas_call(
        sample_kernel,
        out_shape=jax.ShapeDtypeStruct((POOL, 2 * VEC), F32),
        in_specs=[vmem] * 5 + [pl.BlockSpec(memory_space=pltpu.SMEM)],
        out_specs=vmem,
        scratch_shapes=[
            pltpu.VMEM((256, 128), BF16),
            pltpu.VMEM((gath_rows, 128), BF16),
            pltpu.VMEM((ROWS, 128), BF16),
            pltpu.VMEM((ROWS, UNIT), F32),
            pltpu.VMEM((ROWS, UNIT), BF16),
            pltpu.VMEM((ROWS, UNIT), BF16),
            pltpu.VMEM((ROWS, 2 * VEC), F32),
            pltpu.VMEM((SK, 2 * VEC), F32),
            pltpu.VMEM((LEVELS, 8, 2 * SK), F32),
            pltpu.VMEM((LEVELS, 8, 2 * SK), F32),
            pltpu.VMEM((POOL, 2 * VEC), F32),
            dma,
            dma((8,)),
            dma((n_groups,)),
            dma((n_groups, 32)),
            dma((LEVELS,)),
            dma((LEVELS,)),
            dma((3,)),
            dma((3,)),
        ],
        compiler_params=pltpu.CompilerParams(collective_id=1, has_side_effects=True, vmem_limit_bytes=40 << 20),
        name="sample_rows",
    )(row_points, panel_points, test_vectors, leaf_skeleton, node_skeleton[0], leaf_skeleton)


SPREAD = 1.0 + SK / RIDGE
NEWTON = 7


def solve_kernel(pool_ref, nskel_s, interp_ref, maps_ref, top_ref, stacks, skels):
    row = lax.axis_index("rows")
    for lev in range(LEVELS):
        bit = (row // (1 << lev)) % 2
        lower = pl.ds(pl.multiple_of(bit * SK, SK), SK)
        upper = pl.ds(pl.multiple_of((1 - bit) * SK, SK), SK)
        own = pool_ref[HALF : HALF + SK] if lev == 0 else skels[lev - 1]
        stacks[lev, lower] = own
        stacks[lev, upper] = pool_ref[HALF + (lev + 1) * SK : HALF + (lev + 2) * SK]
        for k in range(SK):
            skels[lev, k : k + 1] = stacks[lev, pl.ds(nskel_s[lev, k], 1)]
    top_ref[0] = skels[LEVELS - 1]

    systems = [(pool_ref[HALF : HALF + SK], pool_ref[0:HALF])]
    systems += [(skels[lev], stacks[lev]) for lev in range(LEVELS)]
    eye = (
        lax.broadcasted_iota(jnp.int32, (SK, SK), 0) == lax.broadcasted_iota(jnp.int32, (SK, SK), 1)
    ).astype(F32)

    def mm(p, q):
        return jnp.dot(p, q, precision=HI, preferred_element_type=F32)

    work = []
    for skel, block in systems:
        gram = lax.dot_general(skel, skel, NT, precision=HI, preferred_element_type=F32)
        right = lax.dot_general(skel, block, NT, precision=HI, preferred_element_type=F32)
        mean = jnp.sum(skel * skel) / (SK * 2 * VEC)
        lam = RIDGE * 2 * VEC * (mean + EPSILON)
        scale = 2.0 / ((SPREAD + 1.0) * lam)
        work.append((gram * scale + (2.0 / (SPREAD + 1.0)) * eye, right * scale))
    err = (SPREAD - 1.0) / (SPREAD + 1.0)
    inverses = [eye] * len(work)
    prods = [m for m, _ in work]
    for it in range(NEWTON):
        factor = 2.0 / (2.0 - err * err)
        err = err * err / (2.0 - err * err)
        next_inv, next_prod = [], []
        for inv, prod in zip(inverses, prods):
            left = (2.0 * eye - prod) * factor
            next_inv.append(left if it == 0 else mm(left, inv))
            next_prod.append(mm(left, prod) if it + 1 < NEWTON else prod)
        inverses, prods = next_inv, next_prod
    sols = [mm(inv, right) for inv, (_, right) in zip(inverses, work)]
    rest = [right - mm(m, sol) for sol, (m, right) in zip(sols, work)]
    sols = [sol + mm(inv, r) for sol, inv, r in zip(sols, inverses, rest)]
    interp_ref[...] = sols[0]
    for lev in range(LEVELS):
        maps_ref[0, lev] = sols[lev + 1]


def solve(pool, node_skeleton):
    vmem = pl.BlockSpec(memory_space=pltpu.VMEM)
    return pl.pallas_call(
        solve_kernel,
        out_shape=(
            jax.ShapeDtypeStruct((SK, HALF), F32),
            jax.ShapeDtypeStruct((1, LEVELS, SK, 2 * SK), F32),
            jax.ShapeDtypeStruct((1, SK, 2 * VEC), F32),
        ),
        in_specs=[vmem, pl.BlockSpec(memory_space=pltpu.SMEM)],
        out_specs=(vmem, vmem, vmem),
        scratch_shapes=[pltpu.VMEM((LEVELS, 2 * SK, 2 * VEC), F32), pltpu.VMEM((LEVELS, SK, 2 * VEC), F32)],
        compiler_params=pltpu.CompilerParams(vmem_limit_bytes=40 << 20),
        name="solve",
    )(pool, node_skeleton[0])


def body(row_points, panel_points, test_vectors, leaf_skeleton, node_skeleton):
    pool = sample_rows(row_points, panel_points, test_vectors, leaf_skeleton, node_skeleton)
    return solve(pool, node_skeleton)


def solution(mesh):
    placed = (
        P(None, "rows"),
        P(None, ("rows", "cols")),
        P(None, ("rows", "cols")),
        P("rows", None),
        P("rows", None, None),
    )
    return jax.shard_map(
        body,
        mesh=mesh,
        in_specs=placed,
        out_specs=(P(None, ("rows", "cols")), P("rows", None, None, None), P("rows", None, None)),
        check_vma=False,
    )
```

```python
import functools
import math

import jax
import jax.numpy as jnp
from jax import lax
from jax.experimental import pallas as pl
from jax.experimental.pallas import tpu as pltpu
from jax.sharding import PartitionSpec as P

KAPPA = 40.0
SMOOTH = 0.05
RIDGE = 0.1
EPSILON = 1e-05

MESH = pl.DeviceIdType.MESH
HI = lax.Precision.HIGHEST
NT = (((1,), (1,)), ((), ()))
F32 = jnp.float32
BF16 = jnp.bfloat16

NX, NZ, NY = 4, 8, 8
LEAF = 512
VEC = 128
SK = 64
LEVELS = 4
TREE = LEVELS * SK
ROWS = LEAF + TREE
HALF = LEAF // 2
POOL = HALF + SK + TREE
UNIT = 512
UNITS = 8
EARLY = 4
AHEAD = 4

TURNS = KAPPA / (2.0 * math.pi)
SIN_C = (4.442867902958649, -7.307443418384947, 3.5947880506885697, -0.7843739567847821)
COS_C = (1.414204080778755, -6.977642063413481, 5.7152384214203416, -1.728348662706757)


def horner(q, coefs):
    out = q * coefs[-1] + coefs[-2]
    for c in coefs[-3::-1]:
        out = out * q + c
    return out


def kernel_values(dist_sq):
    inv = lax.rsqrt(dist_sq)
    turns = (dist_sq * inv) * TURNS
    frac = turns - jnp.round(turns)
    q = frac * frac
    sin_half = horner(q, SIN_C) * frac
    cos_half = horner(q, COS_C)
    scaled = inv * sin_half
    return (inv - scaled * sin_half).astype(BF16), (scaled * cos_half).astype(BF16)


def split3(v):
    hi = v.astype(BF16).astype(F32)
    mid = (v - hi).astype(BF16).astype(F32)
    lo = (v - hi - mid).astype(BF16).astype(F32)
    return hi, mid, lo


def stack_rows(rows, width):
    idx = lax.broadcasted_iota(jnp.int32, (16, width), 0)
    out = jnp.zeros((16, width), F32)
    for i, r in enumerate(rows):
        out = jnp.where(idx == i, jnp.broadcast_to(r, (16, width)), out)
    return out


def source_features(points):
    y = [points[i : i + 1, :] for i in range(3)]
    norm = split3(y[0] * y[0] + y[1] * y[1] + y[2] * y[2])
    one = jnp.ones_like(y[0])
    return stack_rows(y * 3 + list(norm) + [one] * 3, points.shape[1])


def target_features(points):
    x = [points[i : i + 1, :] for i in range(3)]
    parts = [split3(-2.0 * v) for v in x]
    norm = split3(x[0] * x[0] + x[1] * x[1] + x[2] * x[2] + SMOOTH * SMOOTH)
    one = jnp.ones_like(x[0])
    rows = [parts[k][s] for s in range(3) for k in range(3)]
    return stack_rows(rows + [one] * 3 + list(norm), points.shape[1])


def target_rows(points):
    feats = target_features(points)
    return jnp.concatenate([feats] * 8, axis=0).T.astype(BF16)


def pick_points(points, picks):
    n = points.shape[1]
    hot = (lax.broadcasted_iota(jnp.int32, (n, SK), 0) == picks).astype(BF16)
    parts = jnp.concatenate(split3(points), axis=0).astype(BF16)
    got = jnp.dot(parts, hot, preferred_element_type=F32)
    return (got[0:8] + got[8:16]) + got[16:24]


BLOCK = 144
LINE = (4, 3, 5, 2, 6, 1, 7)


PLANE = sorted(
    [(i, k) for i in range(NX) for k in range(NZ)],
    key=lambda t: min(t[0], NX - t[0]) + min(t[1], NZ - t[1]),
)


def sample_kernel(
    pts_hbm, panel_ref, vec_hbm, lskel_hbm, nskel_hbm, out_ref,
    pts_ref, lskel_ref, nskel_ref, lskel_s,
    raw, gath, feat_s, vec_s, tgt, u_s, k_re, k_im, acc, own_s, swap_tx, swap_rx, rx,
    raw_send, raw_recv, g_send, g_recv, t_send, t_recv, x_send, x_recv, in_sem,
):
    row = lax.axis_index("rows")
    col = lax.axis_index("cols")
    x, z, y = row // 64, (row // 8) % 8, row % 8
    first = col == 0
    a = jnp.where(first, y, z)
    b = jnp.where(first, z, y)
    step_a = jnp.where(first, 1, 8)
    step_b = jnp.where(first, 8, 1)

    def wrapped(at, by, n):
        return jnp.where(at + by >= n, at + by - n, at + by)

    line = {j: {"rows": row + (wrapped(a, j, 8) - a) * step_a} for j in LINE}
    hop_x = [(wrapped(x, i, NX) - x) * 64 for i in range(NX)]
    hop_b = [(wrapped(b, k, NZ) - b) * step_b for k in range(NZ)]
    plane = [{"rows": row + hop_x[i] + hop_b[k]} for i, k in PLANE]

    barrier = pltpu.get_barrier_semaphore()
    peers = list(line.values()) + plane[1:] + [{"cols": 1 - col}]
    for peer in peers:
        pl.semaphore_signal(barrier, inc=1, device_id=peer, device_id_type=MESH)

    mine = pl.ds(pl.multiple_of(a * 32, 32), 16)
    loads = [
        pltpu.make_async_copy(src, dst, in_sem.at[i])
        for i, (src, dst) in enumerate(
            ((vec_hbm, raw.at[mine]), (pts_hbm, pts_ref), (lskel_hbm, lskel_ref), (nskel_hbm, nskel_ref), (lskel_hbm, lskel_s))
        )
    ]
    for load in loads:
        load.start()

    eye = (
        lax.broadcasted_iota(jnp.int32, (16, 16), 0) == lax.broadcasted_iota(jnp.int32, (16, 16), 1)
    ).astype(BF16)
    mine_f = pl.ds(pl.multiple_of(a * 32 + 16, 16), 16)
    mine_both = pl.ds(pl.multiple_of(a * 32, 32), 32)
    feats = jnp.concatenate([source_features(panel_ref[...].astype(F32))] * 8, axis=0)
    slot = lax.broadcasted_iota(jnp.int32, (128, 16), 0) // 16
    feats = jnp.where(slot == a, feats, 0.0).astype(BF16)
    raw[mine_f] = lax.dot_general(eye, feats, NT, preferred_element_type=F32).astype(BF16)

    loads[0].wait()
    pl.semaphore_wait(barrier, len(peers))

    def raw_copy(j):
        return pltpu.make_async_remote_copy(
            raw.at[mine_both], raw.at[mine_both], raw_send, raw_recv.at[j], device_id=line[j], device_id_type=MESH
        )

    for j in LINE:
        raw_copy(j).start()

    for load in loads[1:]:
        load.wait()

    def swap_copy(lev):
        bit = (row // (1 << lev)) % 2
        return pltpu.make_async_remote_copy(
            swap_tx.at[lev], swap_rx.at[lev], t_send.at[lev], t_recv.at[lev],
            device_id={"rows": row + (1 - 2 * bit) * (1 << lev)}, device_id_type=MESH,
        )

    def swap_start(lev, cur):
        bit = (row // (1 << lev)) % 2
        wide = jnp.concatenate([cur, cur], axis=1)
        upper = lax.broadcasted_iota(jnp.int32, (8, 2 * SK), 1) // SK
        swap_tx[lev] = jnp.where(upper == bit, wide, 0.0)
        swap_copy(lev).start()

    def swap_finish(lev):
        swap_copy(lev).wait_recv()
        bit = (row // (1 << lev)) % 2
        got = swap_rx[lev]
        other = jnp.where(bit == 1, got[:, :SK], got[:, SK:])
        tgt[LEAF + lev * SK : LEAF + (lev + 1) * SK] = target_rows(other)
        both = swap_tx[lev] + got
        if lev + 1 < LEVELS:
            swap_start(lev + 1, pick_points(both, nskel_ref[lev : lev + 1, :]))

    zero_row = jnp.zeros((5, LEAF), F32)
    points = jnp.concatenate([pts_ref[...], zero_row], axis=0)
    swap_start(0, pick_points(points, lskel_ref[...]))
    tgt[0:LEAF] = target_rows(pts_ref[...])
    acc[...] = jnp.zeros_like(acc)

    lane = lax.broadcasted_iota(jnp.int32, (16, 128), 1) // 16

    def block_copy(n, dev):
        return pltpu.make_async_remote_copy(
            gath.at[pl.ds(0, BLOCK)], gath.at[pl.ds(pl.multiple_of(n * BLOCK, 16), BLOCK)], g_send, g_recv.at[n],
            device_id=dev, device_id_type=MESH,
        )

    swap_finish(0)
    for j in LINE:
        raw_copy(j).wait_recv()
    feat = jnp.zeros((16, 128), BF16)
    for i in range(8):
        gath[16 * i : 16 * i + 16] = raw[32 * i : 32 * i + 16]
        feat = feat + raw[32 * i + 16 : 32 * i + 32]
    gath[128:144] = feat
    per_unit = UNIT // 128

    def send_unit(unit):
        for n in range(max(1, unit * per_unit), (unit + 1) * per_unit):
            block_copy(n, plane[n]).start()

    for unit in range(AHEAD):
        send_unit(unit)
    swap_finish(1)

    def fetch(unit):
        for s in range(per_unit):
            n = unit * per_unit + s

            @pl.when(n > 0)
            def _(n=n):
                block_copy(n, plane[1]).wait_recv()

            at = pl.multiple_of(n * BLOCK, 16)
            here = pl.multiple_of(unit * UNIT + s * 128, 128)
            vec_s[pl.ds(here, 128)] = gath[pl.ds(at, 128)]
            tile = gath[pl.ds(pl.multiple_of(at + 128, 16), 16)]
            feat_s[pl.ds(here, 128)] = jnp.concatenate(
                [jnp.where(lane == j, tile, jnp.zeros_like(tile)) for j in range(8)], axis=0
            )

    def add_unit(unit, lo, hi):
        cols = pl.ds(pl.multiple_of(unit * UNIT, UNIT), UNIT)
        vec = vec_s[cols]
        u_s[lo:hi] = lax.dot_general(tgt[lo:hi], feat_s[cols], NT, preferred_element_type=F32)
        for r in range(lo, hi, 16):
            re, im = kernel_values(u_s[r : r + 16])
            k_re[r : r + 16] = re
            k_im[r : r + 16] = im
        acc[lo:hi, :VEC] += jnp.dot(k_re[lo:hi], vec, preferred_element_type=F32)
        acc[lo:hi, VEC:] += jnp.dot(k_im[lo:hi], vec, preferred_element_type=F32)

    def leaf_unit(unit, carry):
        for u in range(EARLY):
            if u + AHEAD < UNITS:
                @pl.when(unit == u)
                def _(u=u):
                    send_unit(u + AHEAD)
        fetch(unit)
        add_unit(unit, 0, LEAF)
        for lev, after in ((2, 0), (3, EARLY - 1)):
            @pl.when(unit == after)
            def _(lev=lev):
                swap_finish(lev)
        return carry

    def tree_unit(unit, carry):
        for u in range(EARLY + AHEAD, UNITS):
            @pl.when(unit == u - EARLY - AHEAD)
            def _(u=u):
                send_unit(u)
        add_unit(unit, LEAF, ROWS)
        return carry

    def full_unit(unit, carry):
        fetch(unit)
        add_unit(unit, 0, ROWS)
        return carry

    lax.fori_loop(0, EARLY, leaf_unit, 0)
    lax.fori_loop(0, EARLY, tree_unit, 0)
    lax.fori_loop(EARLY, UNITS, full_unit, 0)

    for k in range(SK):
        own_s[k : k + 1] = acc[pl.ds(lskel_s[0, k], 1)]
    theirs = pl.ds(pl.multiple_of((1 - col) * HALF, HALF), HALF)
    ours = pl.ds(pl.multiple_of(col * HALF, HALF), HALF)
    spans = (
        (acc.at[theirs], rx.at[pl.ds(0, HALF)]),
        (own_s, rx.at[pl.ds(HALF, SK)]),
        (acc.at[pl.ds(LEAF, TREE)], rx.at[pl.ds(HALF + SK, TREE)]),
    )
    copies = [
        pltpu.make_async_remote_copy(
            src, dst, x_send.at[i], x_recv.at[i], device_id={"cols": 1 - col}, device_id_type=MESH
        )
        for i, (src, dst) in enumerate(spans)
    ]
    for c in copies:
        c.start()
    for c in copies:
        c.wait_recv()
    out_ref[0:HALF] = acc[ours] + rx[0:HALF]
    out_ref[HALF : HALF + SK] = own_s[...] + rx[HALF : HALF + SK]
    out_ref[HALF + SK : POOL] = acc[LEAF:ROWS] + rx[HALF + SK : POOL]

    for c in copies:
        c.wait_send()
    for lev in range(LEVELS):
        swap_copy(lev).wait_send()
    for j in LINE:
        raw_copy(j).wait_send()
    for n in range(1, 32):
        block_copy(n, plane[n]).wait_send()


def sample_rows(row_points, panel_points, test_vectors, leaf_skeleton, node_skeleton):
    vmem = pl.BlockSpec(memory_space=pltpu.VMEM)
    hbm = pl.BlockSpec(memory_space=pltpu.HBM)
    dma = pltpu.SemaphoreType.DMA
    return pl.pallas_call(
        sample_kernel,
        out_shape=jax.ShapeDtypeStruct((POOL, 2 * VEC), F32),
        in_specs=[hbm, vmem, hbm, hbm, hbm],
        out_specs=vmem,
        scratch_shapes=[
            pltpu.VMEM(row_points.shape, F32),
            pltpu.VMEM((1, SK), jnp.int32),
            pltpu.VMEM((LEVELS, SK), jnp.int32),
            pltpu.SMEM((1, SK), jnp.int32),
            pltpu.VMEM((256, 128), BF16),
            pltpu.VMEM((32 * BLOCK, 128), BF16),
            pltpu.VMEM((UNITS * UNIT, 128), BF16),
            pltpu.VMEM((UNITS * UNIT, 128), BF16),
            pltpu.VMEM((ROWS, 128), BF16),
            pltpu.VMEM((ROWS, UNIT), F32),
            pltpu.VMEM((ROWS, UNIT), BF16),
            pltpu.VMEM((ROWS, UNIT), BF16),
            pltpu.VMEM((ROWS, 2 * VEC), F32),
            pltpu.VMEM((SK, 2 * VEC), F32),
            pltpu.VMEM((LEVELS, 8, 2 * SK), F32),
            pltpu.VMEM((LEVELS, 8, 2 * SK), F32),
            pltpu.VMEM((POOL, 2 * VEC), F32),
            dma,
            dma((8,)),
            dma,
            dma((32,)),
            dma((LEVELS,)),
            dma((LEVELS,)),
            dma((3,)),
            dma((3,)),
            dma((5,)),
        ],
        compiler_params=pltpu.CompilerParams(collective_id=1, has_side_effects=True, vmem_limit_bytes=40 << 20),
        name="sample_rows",
    )(row_points, panel_points, test_vectors.T, leaf_skeleton, node_skeleton[0])


SPREAD = 1.0 + SK / RIDGE
NEWTON = 7


def solve_kernel(pool_ref, nskel_s, interp_ref, maps_ref, top_ref, stacks, skels):
    row = lax.axis_index("rows")
    for lev in range(LEVELS):
        bit = (row // (1 << lev)) % 2
        lower = pl.ds(pl.multiple_of(bit * SK, SK), SK)
        upper = pl.ds(pl.multiple_of((1 - bit) * SK, SK), SK)
        own = pool_ref[HALF : HALF + SK] if lev == 0 else skels[lev - 1]
        stacks[lev, lower] = own
        stacks[lev, upper] = pool_ref[HALF + (lev + 1) * SK : HALF + (lev + 2) * SK]
        for k in range(SK):
            skels[lev, k : k + 1] = stacks[lev, pl.ds(nskel_s[lev, k], 1)]
    top_ref[0] = skels[LEVELS - 1]

    systems = [(pool_ref[HALF : HALF + SK], pool_ref[0:HALF])]
    systems += [(skels[lev], stacks[lev]) for lev in range(LEVELS)]
    eye = (
        lax.broadcasted_iota(jnp.int32, (SK, SK), 0) == lax.broadcasted_iota(jnp.int32, (SK, SK), 1)
    ).astype(F32)

    def mm(p, q):
        return jnp.dot(p, q, precision=HI, preferred_element_type=F32)

    work = []
    for skel, block in systems:
        gram = lax.dot_general(skel, skel, NT, precision=HI, preferred_element_type=F32)
        right = lax.dot_general(skel, block, NT, precision=HI, preferred_element_type=F32)
        mean = jnp.sum(skel * skel) / (SK * 2 * VEC)
        lam = RIDGE * 2 * VEC * (mean + EPSILON)
        scale = 2.0 / ((SPREAD + 1.0) * lam)
        work.append((gram * scale + (2.0 / (SPREAD + 1.0)) * eye, right * scale))
    err = (SPREAD - 1.0) / (SPREAD + 1.0)
    inverses = [eye] * len(work)
    prods = [m for m, _ in work]
    for it in range(NEWTON):
        factor = 2.0 / (2.0 - err * err)
        err = err * err / (2.0 - err * err)
        next_inv, next_prod = [], []
        for inv, prod in zip(inverses, prods):
            left = (2.0 * eye - prod) * factor
            next_inv.append(left if it == 0 else mm(left, inv))
            next_prod.append(mm(left, prod) if it + 1 < NEWTON else prod)
        inverses, prods = next_inv, next_prod
    sols = [mm(inv, right) for inv, (_, right) in zip(inverses, work)]
    rest = [right - mm(m, sol) for sol, (m, right) in zip(sols, work)]
    sols = [sol + mm(inv, r) for sol, inv, r in zip(sols, inverses, rest)]
    interp_ref[...] = sols[0]
    for lev in range(LEVELS):
        maps_ref[0, lev] = sols[lev + 1]


def solve(pool, node_skeleton):
    vmem = pl.BlockSpec(memory_space=pltpu.VMEM)
    return pl.pallas_call(
        solve_kernel,
        out_shape=(
            jax.ShapeDtypeStruct((SK, HALF), F32),
            jax.ShapeDtypeStruct((1, LEVELS, SK, 2 * SK), F32),
            jax.ShapeDtypeStruct((1, SK, 2 * VEC), F32),
        ),
        in_specs=[vmem, pl.BlockSpec(memory_space=pltpu.SMEM)],
        out_specs=(vmem, vmem, vmem),
        scratch_shapes=[pltpu.VMEM((LEVELS, 2 * SK, 2 * VEC), F32), pltpu.VMEM((LEVELS, SK, 2 * VEC), F32)],
        compiler_params=pltpu.CompilerParams(vmem_limit_bytes=40 << 20),
        name="solve",
    )(pool, node_skeleton[0])


def body(row_points, panel_points, test_vectors, leaf_skeleton, node_skeleton):
    pool = sample_rows(row_points, panel_points, test_vectors, leaf_skeleton, node_skeleton)
    return solve(pool, node_skeleton)


def solution(mesh):
    placed = (
        P(None, "rows"),
        P(None, ("rows", "cols")),
        P(None, ("rows", "cols")),
        P("rows", None),
        P("rows", None, None),
    )
    return jax.shard_map(
        body,
        mesh=mesh,
        in_specs=placed,
        out_specs=(P(None, ("rows", "cols")), P("rows", None, None, None), P("rows", None, None)),
        check_vma=False,
    )
```

```python
import functools
import math

import jax
import jax.numpy as jnp
from jax import lax
from jax.experimental import pallas as pl
from jax.experimental.pallas import tpu as pltpu
from jax.sharding import PartitionSpec as P

KAPPA = 40.0
SMOOTH = 0.05
RIDGE = 0.1
EPSILON = 1e-05

MESH = pl.DeviceIdType.MESH
HI = lax.Precision.HIGHEST
NT = (((1,), (1,)), ((), ()))
F32 = jnp.float32
BF16 = jnp.bfloat16

NX, NZ, NY = 4, 8, 8
LEAF = 512
VEC = 128
SK = 64
LEVELS = 4
TREE = LEVELS * SK
ROWS = LEAF + TREE
HALF = LEAF // 2
POOL = HALF + SK + TREE
UNIT = 512
UNITS = 8
EARLY = 4
AHEAD = 4

TURNS = KAPPA / (2.0 * math.pi)
SIN_C = (4.442867902958649, -7.307443418384947, 3.5947880506885697, -0.7843739567847821)
COS_C = (1.414204080778755, -6.977642063413481, 5.7152384214203416, -1.728348662706757)


def horner(q, coefs):
    out = q * coefs[-1] + coefs[-2]
    for c in coefs[-3::-1]:
        out = out * q + c
    return out


def kernel_values(dist_sq):
    inv = lax.rsqrt(dist_sq)
    turns = (dist_sq * inv) * TURNS
    frac = turns - jnp.round(turns)
    q = frac * frac
    sin_half = horner(q, SIN_C) * frac
    cos_half = horner(q, COS_C)
    scaled = inv * sin_half
    return (inv - scaled * sin_half).astype(BF16), (scaled * cos_half).astype(BF16)


def split3(v):
    hi = v.astype(BF16).astype(F32)
    mid = (v - hi).astype(BF16).astype(F32)
    lo = (v - hi - mid).astype(BF16).astype(F32)
    return hi, mid, lo


def stack_rows(rows, width):
    idx = lax.broadcasted_iota(jnp.int32, (16, width), 0)
    out = jnp.zeros((16, width), F32)
    for i, r in enumerate(rows):
        out = jnp.where(idx == i, jnp.broadcast_to(r, (16, width)), out)
    return out


def source_features(points):
    y = [points[i : i + 1, :] for i in range(3)]
    norm = split3(y[0] * y[0] + y[1] * y[1] + y[2] * y[2])
    one = jnp.ones_like(y[0])
    return stack_rows(y * 3 + list(norm) + [one] * 3, points.shape[1])


def target_features(points):
    x = [points[i : i + 1, :] for i in range(3)]
    parts = [split3(-2.0 * v) for v in x]
    norm = split3(x[0] * x[0] + x[1] * x[1] + x[2] * x[2] + SMOOTH * SMOOTH)
    one = jnp.ones_like(x[0])
    rows = [parts[k][s] for s in range(3) for k in range(3)]
    return stack_rows(rows + [one] * 3 + list(norm), points.shape[1])


def target_rows(points):
    feats = target_features(points)
    return jnp.concatenate([feats] * 8, axis=0).T.astype(BF16)


def pick_points(points, picks):
    n = points.shape[1]
    hot = (lax.broadcasted_iota(jnp.int32, (n, SK), 0) == picks).astype(BF16)
    parts = jnp.concatenate(split3(points), axis=0).astype(BF16)
    got = jnp.dot(parts, hot, preferred_element_type=F32)
    return (got[0:8] + got[8:16]) + got[16:24]


BLOCK = 144
LINE = (4, 3, 5, 2, 6, 1, 7)


PLANE = sorted(
    [(i, k) for i in range(NX) for k in range(NZ)],
    key=lambda t: min(t[0], NX - t[0]) + min(t[1], NZ - t[1]),
)


def sample_kernel(
    pts_hbm, panel_ref, vec_ref, lskel_hbm, nskel_hbm, out_ref,
    pts_ref, lskel_ref, nskel_ref, lskel_s,
    raw, gath, feat_s, vec_s, tgt, u_s, k_re, k_im, acc, own_s, swap_tx, swap_rx, rx,
    raw_send, raw_recv, g_send, g_recv, t_send, t_recv, x_send, x_recv, in_sem,
):
    row = lax.axis_index("rows")
    col = lax.axis_index("cols")
    x, z, y = row // 64, (row // 8) % 8, row % 8
    first = col == 0
    a = jnp.where(first, y, z)
    b = jnp.where(first, z, y)
    step_a = jnp.where(first, 1, 8)
    step_b = jnp.where(first, 8, 1)

    def wrapped(at, by, n):
        return jnp.where(at + by >= n, at + by - n, at + by)

    line = {j: {"rows": row + (wrapped(a, j, 8) - a) * step_a} for j in LINE}
    hop_x = [(wrapped(x, i, NX) - x) * 64 for i in range(NX)]
    hop_b = [(wrapped(b, k, NZ) - b) * step_b for k in range(NZ)]
    plane = [{"rows": row + hop_x[i] + hop_b[k]} for i, k in PLANE]

    barrier = pltpu.get_barrier_semaphore()
    peers = list(line.values()) + plane[1:] + [{"cols": 1 - col}]
    for peer in peers:
        pl.semaphore_signal(barrier, inc=1, device_id=peer, device_id_type=MESH)

    mine = pl.ds(pl.multiple_of(a * 32, 32), 16)
    loads = [
        pltpu.make_async_copy(src, dst, in_sem.at[i])
        for i, (src, dst) in enumerate(
            ((pts_hbm, pts_ref), (lskel_hbm, lskel_ref), (nskel_hbm, nskel_ref), (lskel_hbm, lskel_s))
        )
    ]
    for load in loads:
        load.start()

    eye = (
        lax.broadcasted_iota(jnp.int32, (16, 16), 0) == lax.broadcasted_iota(jnp.int32, (16, 16), 1)
    ).astype(BF16)
    mine_f = pl.ds(pl.multiple_of(a * 32 + 16, 16), 16)
    mine_both = pl.ds(pl.multiple_of(a * 32, 32), 32)
    feats = jnp.concatenate([source_features(panel_ref[...].astype(F32))] * 8, axis=0)
    slot = lax.broadcasted_iota(jnp.int32, (128, 16), 0) // 16
    feats = jnp.where(slot == a, feats, 0.0).astype(BF16)
    raw[mine] = lax.dot_general(eye, vec_ref[...], NT, preferred_element_type=F32).astype(BF16)
    raw[mine_f] = lax.dot_general(eye, feats, NT, preferred_element_type=F32).astype(BF16)

    pl.semaphore_wait(barrier, len(peers))

    def raw_copy(j):
        return pltpu.make_async_remote_copy(
            raw.at[mine_both], raw.at[mine_both], raw_send, raw_recv.at[j], device_id=line[j], device_id_type=MESH
        )

    for j in LINE:
        raw_copy(j).start()

    for load in loads:
        load.wait()

    def swap_copy(lev):
        bit = (row // (1 << lev)) % 2
        return pltpu.make_async_remote_copy(
            swap_tx.at[lev], swap_rx.at[lev], t_send.at[lev], t_recv.at[lev],
            device_id={"rows": row + (1 - 2 * bit) * (1 << lev)}, device_id_type=MESH,
        )

    def swap_start(lev, cur):
        bit = (row // (1 << lev)) % 2
        wide = jnp.concatenate([cur, cur], axis=1)
        upper = lax.broadcasted_iota(jnp.int32, (8, 2 * SK), 1) // SK
        swap_tx[lev] = jnp.where(upper == bit, wide, 0.0)
        swap_copy(lev).start()

    def swap_finish(lev):
        swap_copy(lev).wait_recv()
        bit = (row // (1 << lev)) % 2
        got = swap_rx[lev]
        other = jnp.where(bit == 1, got[:, :SK], got[:, SK:])
        tgt[LEAF + lev * SK : LEAF + (lev + 1) * SK] = target_rows(other)
        both = swap_tx[lev] + got
        if lev + 1 < LEVELS:
            swap_start(lev + 1, pick_points(both, nskel_ref[lev : lev + 1, :]))

    zero_row = jnp.zeros((5, LEAF), F32)
    points = jnp.concatenate([pts_ref[...], zero_row], axis=0)
    swap_start(0, pick_points(points, lskel_ref[...]))
    tgt[0:LEAF] = target_rows(pts_ref[...])
    acc[...] = jnp.zeros_like(acc)

    lane = lax.broadcasted_iota(jnp.int32, (16, 128), 1) // 16

    def block_copy(n, dev):
        return pltpu.make_async_remote_copy(
            gath.at[pl.ds(0, BLOCK)], gath.at[pl.ds(pl.multiple_of(n * BLOCK, 16), BLOCK)], g_send, g_recv.at[n],
            device_id=dev, device_id_type=MESH,
        )

    swap_finish(0)
    for j in LINE:
        raw_copy(j).wait_recv()
    feat = jnp.zeros((16, 128), BF16)
    for i in range(8):
        gath[16 * i : 16 * i + 16] = raw[32 * i : 32 * i + 16]
        feat = feat + raw[32 * i + 16 : 32 * i + 32]
    gath[128:144] = feat
    per_unit = UNIT // 128

    def send_unit(unit):
        for n in range(max(1, unit * per_unit), (unit + 1) * per_unit):
            block_copy(n, plane[n]).start()

    for unit in range(AHEAD):
        send_unit(unit)
    swap_finish(1)

    def fetch(unit):
        for s in range(per_unit):
            n = unit * per_unit + s

            @pl.when(n > 0)
            def _(n=n):
                block_copy(n, plane[1]).wait_recv()

            at = pl.multiple_of(n * BLOCK, 16)
            here = pl.multiple_of(unit * UNIT + s * 128, 128)
            vec_s[pl.ds(here, 128)] = gath[pl.ds(at, 128)]
            tile = gath[pl.ds(pl.multiple_of(at + 128, 16), 16)]
            feat_s[pl.ds(here, 128)] = jnp.concatenate(
                [jnp.where(lane == j, tile, jnp.zeros_like(tile)) for j in range(8)], axis=0
            )

    def add_unit(unit, lo, hi):
        cols = pl.ds(pl.multiple_of(unit * UNIT, UNIT), UNIT)
        vec = vec_s[cols]
        u_s[lo:hi] = lax.dot_general(tgt[lo:hi], feat_s[cols], NT, preferred_element_type=F32)
        for r in range(lo, hi, 16):
            re, im = kernel_values(u_s[r : r + 16])
            k_re[r : r + 16] = re
            k_im[r : r + 16] = im
        acc[lo:hi, :VEC] += jnp.dot(k_re[lo:hi], vec, preferred_element_type=F32)
        acc[lo:hi, VEC:] += jnp.dot(k_im[lo:hi], vec, preferred_element_type=F32)

    def leaf_unit(unit, carry):
        for u in range(EARLY):
            if u + AHEAD < UNITS:
                @pl.when(unit == u)
                def _(u=u):
                    send_unit(u + AHEAD)
        fetch(unit)
        add_unit(unit, 0, LEAF)
        for lev, after in ((2, 0), (3, EARLY - 1)):
            @pl.when(unit == after)
            def _(lev=lev):
                swap_finish(lev)
        return carry

    def tree_unit(unit, carry):
        for u in range(EARLY + AHEAD, UNITS):
            @pl.when(unit == u - EARLY - AHEAD)
            def _(u=u):
                send_unit(u)
        add_unit(unit, LEAF, ROWS)
        return carry

    def full_unit(unit, carry):
        fetch(unit)
        add_unit(unit, 0, ROWS)
        return carry

    lax.fori_loop(0, EARLY, leaf_unit, 0)
    lax.fori_loop(0, EARLY, tree_unit, 0)
    lax.fori_loop(EARLY, UNITS, full_unit, 0)

    for k in range(SK):
        own_s[k : k + 1] = acc[pl.ds(lskel_s[0, k], 1)]
    theirs = pl.ds(pl.multiple_of((1 - col) * HALF, HALF), HALF)
    ours = pl.ds(pl.multiple_of(col * HALF, HALF), HALF)
    spans = (
        (acc.at[theirs], rx.at[pl.ds(0, HALF)]),
        (own_s, rx.at[pl.ds(HALF, SK)]),
        (acc.at[pl.ds(LEAF, TREE)], rx.at[pl.ds(HALF + SK, TREE)]),
    )
    copies = [
        pltpu.make_async_remote_copy(
            src, dst, x_send.at[i], x_recv.at[i], device_id={"cols": 1 - col}, device_id_type=MESH
        )
        for i, (src, dst) in enumerate(spans)
    ]
    for c in copies:
        c.start()
    for c in copies:
        c.wait_recv()
    out_ref[0:HALF] = acc[ours] + rx[0:HALF]
    out_ref[HALF : HALF + SK] = own_s[...] + rx[HALF : HALF + SK]
    out_ref[HALF + SK : POOL] = acc[LEAF:ROWS] + rx[HALF + SK : POOL]

    for c in copies:
        c.wait_send()
    for lev in range(LEVELS):
        swap_copy(lev).wait_send()
    for j in LINE:
        raw_copy(j).wait_send()
    for n in range(1, 32):
        block_copy(n, plane[n]).wait_send()


def sample_rows(row_points, panel_points, test_vectors, leaf_skeleton, node_skeleton):
    vmem = pl.BlockSpec(memory_space=pltpu.VMEM)
    hbm = pl.BlockSpec(memory_space=pltpu.HBM)
    dma = pltpu.SemaphoreType.DMA
    return pl.pallas_call(
        sample_kernel,
        out_shape=jax.ShapeDtypeStruct((POOL, 2 * VEC), F32),
        in_specs=[hbm, vmem, vmem, hbm, hbm],
        out_specs=vmem,
        scratch_shapes=[
            pltpu.VMEM(row_points.shape, F32),
            pltpu.VMEM((1, SK), jnp.int32),
            pltpu.VMEM((LEVELS, SK), jnp.int32),
            pltpu.SMEM((1, SK), jnp.int32),
            pltpu.VMEM((256, 128), BF16),
            pltpu.VMEM((32 * BLOCK, 128), BF16),
            pltpu.VMEM((UNITS * UNIT, 128), BF16),
            pltpu.VMEM((UNITS * UNIT, 128), BF16),
            pltpu.VMEM((ROWS, 128), BF16),
            pltpu.VMEM((ROWS, UNIT), F32),
            pltpu.VMEM((ROWS, UNIT), BF16),
            pltpu.VMEM((ROWS, UNIT), BF16),
            pltpu.VMEM((ROWS, 2 * VEC), F32),
            pltpu.VMEM((SK, 2 * VEC), F32),
            pltpu.VMEM((LEVELS, 8, 2 * SK), F32),
            pltpu.VMEM((LEVELS, 8, 2 * SK), F32),
            pltpu.VMEM((POOL, 2 * VEC), F32),
            dma,
            dma((8,)),
            dma,
            dma((32,)),
            dma((LEVELS,)),
            dma((LEVELS,)),
            dma((3,)),
            dma((3,)),
            dma((4,)),
        ],
        compiler_params=pltpu.CompilerParams(collective_id=1, has_side_effects=True, vmem_limit_bytes=40 << 20),
        name="sample_rows",
    )(row_points, panel_points, test_vectors, leaf_skeleton, node_skeleton[0])


SPREAD = 1.0 + SK / RIDGE
NEWTON = 7


def solve_kernel(pool_ref, nskel_s, interp_ref, maps_ref, top_ref, stacks, skels):
    row = lax.axis_index("rows")
    for lev in range(LEVELS):
        bit = (row // (1 << lev)) % 2
        lower = pl.ds(pl.multiple_of(bit * SK, SK), SK)
        upper = pl.ds(pl.multiple_of((1 - bit) * SK, SK), SK)
        own = pool_ref[HALF : HALF + SK] if lev == 0 else skels[lev - 1]
        stacks[lev, lower] = own
        stacks[lev, upper] = pool_ref[HALF + (lev + 1) * SK : HALF + (lev + 2) * SK]
        for k in range(SK):
            skels[lev, k : k + 1] = stacks[lev, pl.ds(nskel_s[lev, k], 1)]
    top_ref[0] = skels[LEVELS - 1]

    systems = [(pool_ref[HALF : HALF + SK], pool_ref[0:HALF])]
    systems += [(skels[lev], stacks[lev]) for lev in range(LEVELS)]
    eye = (
        lax.broadcasted_iota(jnp.int32, (SK, SK), 0) == lax.broadcasted_iota(jnp.int32, (SK, SK), 1)
    ).astype(F32)

    def mm(p, q):
        return jnp.dot(p, q, precision=HI, preferred_element_type=F32)

    def halves(p):
        hi = p.astype(BF16)
        return hi, (p - hi.astype(F32)).astype(BF16)

    def mm3(p, q):
        (ph, pl_), (qh, ql) = p, q
        dot = functools.partial(jnp.dot, preferred_element_type=F32)
        return dot(ph, qh) + (dot(ph, ql) + dot(pl_, qh))

    work = []
    for skel, block in systems:
        gram = lax.dot_general(skel, skel, NT, precision=HI, preferred_element_type=F32)
        right = lax.dot_general(skel, block, NT, precision=HI, preferred_element_type=F32)
        mean = jnp.sum(skel * skel) / (SK * 2 * VEC)
        lam = RIDGE * 2 * VEC * (mean + EPSILON)
        scale = 2.0 / ((SPREAD + 1.0) * lam)
        work.append((gram * scale + (2.0 / (SPREAD + 1.0)) * eye, right * scale))
    err = (SPREAD - 1.0) / (SPREAD + 1.0)
    inverses = [eye] * len(work)
    prods = [m for m, _ in work]
    for it in range(NEWTON):
        factor = 2.0 / (2.0 - err * err)
        err = err * err / (2.0 - err * err)
        next_inv, next_prod = [], []
        for inv, prod in zip(inverses, prods):
            left = (2.0 * eye - prod) * factor
            parts = halves(left)
            next_inv.append(left if it == 0 else mm3(parts, halves(inv)))
            next_prod.append(mm3(parts, halves(prod)) if it + 1 < NEWTON else prod)
        inverses, prods = next_inv, next_prod
    inverses = [halves(inv) for inv in inverses]
    sols = [mm3(inv, halves(right)) for inv, (_, right) in zip(inverses, work)]
    rest = [right - mm(m, sol) for sol, (m, right) in zip(sols, work)]
    sols = [sol + mm3(inv, halves(r)) for sol, inv, r in zip(sols, inverses, rest)]
    interp_ref[...] = sols[0]
    for lev in range(LEVELS):
        maps_ref[0, lev] = sols[lev + 1]


def solve(pool, node_skeleton):
    vmem = pl.BlockSpec(memory_space=pltpu.VMEM)
    return pl.pallas_call(
        solve_kernel,
        out_shape=(
            jax.ShapeDtypeStruct((SK, HALF), F32),
            jax.ShapeDtypeStruct((1, LEVELS, SK, 2 * SK), F32),
            jax.ShapeDtypeStruct((1, SK, 2 * VEC), F32),
        ),
        in_specs=[vmem, pl.BlockSpec(memory_space=pltpu.SMEM)],
        out_specs=(vmem, vmem, vmem),
        scratch_shapes=[pltpu.VMEM((LEVELS, 2 * SK, 2 * VEC), F32), pltpu.VMEM((LEVELS, SK, 2 * VEC), F32)],
        compiler_params=pltpu.CompilerParams(vmem_limit_bytes=40 << 20),
        name="solve",
    )(pool, node_skeleton[0])


def body(row_points, panel_points, test_vectors, leaf_skeleton, node_skeleton):
    pool = sample_rows(row_points, panel_points, test_vectors, leaf_skeleton, node_skeleton)
    return solve(pool, node_skeleton)


def solution(mesh):
    placed = (
        P(None, "rows"),
        P(None, ("rows", "cols")),
        P(None, ("rows", "cols")),
        P("rows", None),
        P("rows", None, None),
    )
    return jax.shard_map(
        body,
        mesh=mesh,
        in_specs=placed,
        out_specs=(P(None, ("rows", "cols")), P("rows", None, None, None), P("rows", None, None)),
        check_vma=False,
    )
```
